32 devices in a mesh: grp: 2 (over x), tm: 16 (over z, y, core).
Axes of the slice: x: 2, y: 2, z: 4, core: 2. Of those that a mesh axis runs over, the one named last changes fastest.
Arguments:
- states: float32 [32, 84, 12, 128], P(('grp', 'tm')), parts along dimension 0, may hold values from -6 to 6
- slab_steps: int32 [32], P(('grp', 'tm')), parts along dimension 0, may hold values from 0 to 999
- offset: int32 [2], P('grp'), parts along dimension 0, may hold values from 0 to 999
- log_sigma: float32 [1000], replicated, may hold values from -2 to 2
- step_size: float32 [1000], replicated, may hold values from -0.12 to -0.03
- w_in: bfloat16 [9, 256, 84], replicated, may hold values from -0.21875 to 0.21875
- w_mid: bfloat16 [9, 256, 256], replicated, may hold values from -0.125 to 0.125
- w_out: bfloat16 [9, 84, 256], replicated, may hold values from -0.125 to 0.125
- embed: float32 [256], replicated, may hold values from -5 to 5
Outputs:
- new_states: float32 [32, 84, 12, 128], P(('grp', 'tm')), parts along dimension 0
The draws below stay inside these ranges and needn't reach their ends.
There are 2 independent parts, one for each index of `grp`. The reference program is written for one: setup_inputs(seed, part) draws one part's arguments, and reference() takes and returns one part's arrays. A program takes and returns all parts, laid end to end along the dimension named above; an argument that names none is the same for every part. Nothing has to cross between parts.
All inputs are finite; a program needn't handle non-finite values.
Results may differ from the reference program's by a relative error of at most 0.0011.
Values sent between devices are 32-bit elements; how exact they have to be, the bound alone decides.
A program may use at most 64 MiB of HBM per device.

```python
import jax
import jax.numpy as jnp
from jax import lax

F = 84
CH = 256
H = 12
W = 128
TABLE = 1000
SWEEPS = 2
SLABS = 16


def plant(entries, key, least, largest):
    index_at = [jax.random.randint(jax.random.fold_in(key, axis), (), 0, length) for axis, length in enumerate(entries.shape)]
    longest = entries.shape.index(max(entries.shape))
    neighbour = index_at[:longest] + [(index_at[longest] + 1) % entries.shape[longest]] + index_at[longest + 1:]
    return entries.at[tuple(index_at)].set(least).at[tuple(neighbour)].set(largest)


def steps_of(key, extent, split, low, largest):
    def one(dim, shards_of):
        steps = jax.random.uniform(jax.random.fold_in(jax.random.fold_in(key, 6), dim), (shards_of,), jnp.float32, low / len(split), largest / len(split))
        return jnp.repeat(jnp.exp(steps), extent[dim] // shards_of).reshape((-1,) + (1,) * (len(extent) - dim - 1))

    level = one(*split[0])
    for cut in split[1:]:
        level = level * one(*cut)
    return level


def noise(key, shape, scale, bound, pieces=(), held_as=jnp.bfloat16):
    factor_of = steps_of(key, shape, pieces, -0.22, 0.18) if pieces else 1.0
    values = jax.random.normal(key, shape, jnp.float32) * scale * factor_of
    return jnp.minimum(jnp.maximum(values, -bound), bound).astype(held_as)


def setup_inputs(seed: int = 0, part: int = 0) -> dict:
    keys = jax.random.split(jax.random.key(seed), 10)
    own_keys = jax.random.split(jax.random.fold_in(keys[9], part), 10)
    return {
        "states": noise(own_keys[0], (SLABS, F, H, W), 1.0, 6.0, ((0, 16),), jnp.float32),
        "slab_steps": plant(jax.random.randint(own_keys[1], (SLABS,), 0, TABLE), jax.random.fold_in(own_keys[1], 1), 0, TABLE - 1).astype(jnp.int32),
        "offset": jax.random.randint(own_keys[2], (1,), 0, TABLE).astype(jnp.int32),
        "log_sigma": jnp.clip(jax.random.uniform(keys[3], (TABLE,), jnp.float32, -2.0, 2.0), -2.0, 2.0),
        "step_size": jnp.clip(jax.random.uniform(keys[4], (TABLE,), jnp.float32, -0.12, -0.03), -0.12, -0.03),
        "w_in": noise(keys[5], (9, CH, F), (9 * F) ** -0.5, 0.21875),
        "w_mid": noise(keys[6], (9, CH, CH), (9 * CH) ** -0.5, 0.125),
        "w_out": noise(keys[7], (9, F, CH), (9 * CH) ** -0.5, 0.125),
        "embed": noise(keys[8], (CH,), 1.0, 5.0, (), jnp.float32),
    }


def convolve(field, weights):
    channels = field.shape[0]
    padded = jnp.pad(field, ((0, 0), (1, 1), (1, 1)))
    total = jnp.zeros((weights.shape[1], H * W), jnp.float32)
    for kernel_tap in range(9):
        row_shift = kernel_tap // 3
        col_shift = kernel_tap % 3
        window = padded[:, row_shift:row_shift + H, col_shift:col_shift + W].reshape(channels, H * W)
        total = total + jnp.dot(weights[kernel_tap], window, preferred_element_type=jnp.float32)
    return total


def drift_field(field, log_noise, w_in, w_mid, w_out, embed):
    first = convolve(field.astype(jnp.bfloat16), w_in) + log_noise * embed[:, None]
    first = jax.nn.silu(first).astype(jnp.bfloat16).reshape(CH, H, W)
    second = jax.nn.silu(convolve(first, w_mid)).astype(jnp.bfloat16).reshape(CH, H, W)
    return convolve(second, w_out).reshape(F, H, W)


def reference(states, slab_steps, offset, log_sigma, step_size, w_in, w_mid, w_out, embed):
    table_row = ((slab_steps + offset[0]) % TABLE).astype(jnp.int32)
    log_noise = log_sigma[table_row]
    step_len = step_size[table_row]
    field = states
    through = states
    for sweep_index in range(SWEEPS):
        drifts = lax.map(lambda operands: drift_field(operands[0], operands[1], w_in, w_mid, w_out, embed), (field, log_noise))
        increments = step_len[:, None, None, None] * drifts
        increments = increments.at[0].add(field[0])
        through = jnp.cumsum(increments, axis=0)
        if sweep_index + 1 < SWEEPS:
            field = jnp.concatenate([field[:1], through[:-1]], axis=0)
    return through
```

```python
import functools

import jax
import jax.numpy as jnp
from jax import lax
from jax.experimental import pallas as pl
from jax.experimental.pallas import tpu as pltpu
from jax.sharding import PartitionSpec as P

SWEEPS = 2
MESH = pl.DeviceIdType.MESH


def up(value, multiple):
    return (value + multiple - 1) // multiple * multiple


def kernel(dims, x_hbm, steps_ref, offset_ref, ls_ref, ss_ref, win_hbm, wmid_hbm, wout_hbm, emb_ref, out_ref,
           win_v, wout_v, w1, w2, w3, eb, xf, xc, u1, u2, inc,
           ra, rp, rs, re, rr, sf, sb, se, sr,
           load_sem, wmid_sem, ssem, rsem):
    n, inner, F, CH, H, W, FP = dims
    outer = n // (2 * inner)
    K = H // 2
    me = lax.axis_index("tm")
    core = lax.rem(me, 2)
    chip = me // 2
    b = lax.rem(chip, inner)
    a = chip // inner
    partner = me + 1 - 2 * core
    b_next, b_prev = me + 2, me - 2
    a_next, a_prev = me + 2 * inner, me - 2 * inner

    loads = [
        pltpu.make_async_copy(x_hbm, xf.at[pl.ds(1, H)], load_sem.at[0]),
        pltpu.make_async_copy(win_hbm, win_v, load_sem.at[1]),
        pltpu.make_async_copy(wout_hbm, wout_v, load_sem.at[2]),
    ]
    for tap in range(9):
        ka, kb = tap // 3, tap % 3
        loads.append(
            pltpu.make_async_copy(
                wmid_hbm.at[tap], w2.at[pl.ds(kb * CH, CH), pl.ds(ka * CH, CH)], wmid_sem.at[tap]
            )
        )
    loads[1].start()
    loads[0].start()
    for copy in loads[2:]:
        copy.start()

    @pl.when(b == 0)
    def _():
        rp[...] = jnp.zeros_like(rp)

    @pl.when(b == inner - 1)
    def _():
        rs[...] = jnp.zeros_like(rs)

    @pl.when(a == 0)
    def _():
        re[...] = jnp.zeros_like(re)

    barrier = pltpu.get_barrier_semaphore()

    def greet(device):
        pl.semaphore_signal(barrier, inc=1, device_id={"tm": device}, device_id_type=MESH)

    greet(partner)
    for there, device in ((b > 0, b_prev), (b < inner - 1, b_next), (a > 0, a_prev), (a < outer - 1, a_next)):
        pl.when(there)(functools.partial(greet, device))

    table_row = lax.rem(steps_ref[0] + offset_ref[0], ls_ref.shape[0])
    log_noise = ls_ref[table_row]
    step_len = ss_ref[table_row]
    first = jnp.where(me == 0, 1.0, 0.0).astype(jnp.float32)

    for block in range(CH // 128):
        row = emb_ref[pl.ds(block, 1), :] * log_noise
        eb[pl.ds(block * 128, 128), :] = jnp.transpose(jnp.broadcast_to(row, (128, 128)))
    zero_row = jnp.zeros((CH, W), jnp.bfloat16)
    for edge in (0, H + 1):
        u1[edge] = zero_row
        u2[edge] = zero_row
        xf[edge] = jnp.zeros((F, W), jnp.float32)

    loads[1].wait()
    for kb in range(3):
        parts = [win_v[3 * ka + kb].astype(jnp.float32) for ka in range(3)]
        parts.append(jnp.zeros((CH, w1.shape[1] - 3 * F), jnp.float32))
        w1[pl.ds(kb * CH, CH), :] = jnp.concatenate(parts, axis=1).astype(jnp.bfloat16)
    loads[0].wait()

    lane = lax.broadcasted_iota(jnp.int32, (1, W), 1)

    def combine(product, rows, base, j):
        cols = slice(j * W, (j + 1) * W)
        left = pltpu.roll(product[0:rows, cols], 1, axis=1)
        mid = product[base:base + rows, cols]
        right = pltpu.roll(product[2 * base:2 * base + rows, cols], W - 1, axis=1)
        return mid + jnp.where(lane == 0, 0.0, left) + jnp.where(lane == W - 1, 0.0, right)

    def silu(value):
        half = 0.5 * value
        return half * (1.0 + jnp.tanh(half))

    def stage(r):
        parts = [xf[r], xf[r + 1], xf[r + 2], jnp.zeros((w1.shape[1] - 3 * F, W), jnp.float32)]
        xc[r] = jnp.concatenate(parts, axis=0).astype(jnp.bfloat16)

    def conv1(k):
        r = 2 * k
        stage(r)
        stage(r + 1)
        z = jnp.concatenate([xc[r], xc[r + 1]], axis=1)
        product = jnp.dot(w1[...], z, preferred_element_type=jnp.float32)
        for j in range(2):
            u1[r + j + 1] = silu(combine(product, CH, CH, j) + eb[...]).astype(jnp.bfloat16)

    def taps(u, r):
        return jnp.concatenate(
            [jnp.concatenate([u[r + ka], u[r + ka + 1]], axis=1) for ka in range(3)], axis=0
        )

    def conv2(k):
        r = 2 * k
        product = jnp.dot(w2[...], taps(u1, r), preferred_element_type=jnp.float32)
        for j in range(2):
            u2[r + j + 1] = silu(combine(product, CH, CH, j)).astype(jnp.bfloat16)

    def conv3(s, k):
        r = 2 * k
        product = jnp.dot(w3[...], taps(u2, r), preferred_element_type=jnp.float32)
        for j in range(2):
            inc[s, r + j] = step_len * combine(product, F, FP, j) + first * xf[r + j + 1]

    def remote(kind, s, k, src, dst, device):
        return pltpu.make_async_remote_copy(
            src_ref=src,
            dst_ref=dst,
            send_sem=ssem.at[kind, s, k],
            recv_sem=rsem.at[kind, s, k],
            device_id={"tm": device},
            device_id_type=MESH,
        )

    def own(k):
        return 2 * k + core

    def other(k):
        return 2 * k + 1 - core

    def pair(s, k):
        return remote(0, s, k, inc.at[s, other(k)], ra.at[s, k], partner)

    def forward(s, k):
        return remote(1, s, k, sf.at[s, k], rp.at[s, k], b_next)

    def backward(s, k):
        return remote(2, s, k, sb.at[s, k], rs.at[s, k], b_prev)

    def chain(s, k):
        return remote(3, s, k, se.at[s, k], re.at[s, k], a_next)

    def result(s, k):
        return remote(4, s, k, sr.at[s, k], rr.at[s, k], partner)

    def send_pair(s, k):
        pair(s, k).start()

    def send_chip(s, k):
        pair(s, k).wait_recv()
        chip_sum = inc[s, own(k)] + ra[s, k]
        sf[s, k] = chip_sum
        sb[s, k] = chip_sum

        @pl.when(b == 0)
        def _():
            forward(s, k).start()

        @pl.when(b == inner - 1)
        def _():
            backward(s, k).start()

    def send_plane(s, k):
        middle = (b > 0) & (b < inner - 1)
        chip_sum = inc[s, own(k)] + ra[s, k]

        @pl.when(b > 0)
        def _():
            forward(s, k).wait_recv()

        if inner > 2:
            @pl.when(middle)
            def _():
                sf[s, k] = rp[s, k] + chip_sum
                forward(s, k).start()

        @pl.when(b < inner - 1)
        def _():
            backward(s, k).wait_recv()

        if inner > 2:
            @pl.when(middle)
            def _():
                sb[s, k] = rs[s, k] + chip_sum
                backward(s, k).start()

        @pl.when(a > 0)
        def _():
            chain(s, k).wait_recv()

        before = re[s, k] + rp[s, k]

        @pl.when(a < outer - 1)
        def _():
            se[s, k] = before + chip_sum + rs[s, k]
            chain(s, k).start()

        is_second = core.astype(jnp.float32)
        sr[s, k] = before + (1.0 - is_second) * inc[s, own(k)]
        result(s, k).start()
        finish(s, own(k), before + is_second * ra[s, k])

    def finish(s, r, before):
        if s + 1 < SWEEPS:
            xf[r + 1] = before + first * xf[r + 1]
        else:
            out_ref[r] = before + inc[s, r]

    def receive(s, k):
        result(s, k).wait_recv()
        finish(s, other(k), rr[s, k])

    for s in range(SWEEPS):
        for t in range(K + 2):
            if t < K:
                conv1(t)
            if s == 0 and t == 0:
                for copy in loads[3:]:
                    copy.wait()
            if 1 <= t <= K:
                conv2(t - 1)
            if s == 0 and t == 1:
                loads[2].wait()
                for tap in range(9):
                    ka, kb = tap // 3, tap % 3
                    padded = jnp.concatenate(
                        [wout_v[tap].astype(jnp.float32), jnp.zeros((FP - F, CH), jnp.float32)], axis=0
                    )
                    w3[pl.ds(kb * FP, FP), pl.ds(ka * CH, CH)] = padded.astype(jnp.bfloat16)
                count = 1 + (b > 0).astype(jnp.int32) + (b < inner - 1).astype(jnp.int32)
                count = count + (a > 0).astype(jnp.int32) + (a < outer - 1).astype(jnp.int32)
                pl.semaphore_wait(barrier, count)
            if t >= 2:
                conv3(s, t - 2)
                send_pair(s, t - 2)
            if t >= 3:
                send_chip(s, t - 3)
            if t >= 4:
                send_plane(s, t - 4)
        send_chip(s, K - 1)
        send_plane(s, K - 2)
        send_plane(s, K - 1)
        for k in range(K):
            receive(s, k)

    for s in range(SWEEPS):
        for k in range(K):
            pair(s, k).wait_send()
            pl.when(b < inner - 1)(lambda s=s, k=k: forward(s, k).wait_send())
            pl.when(b > 0)(lambda s=s, k=k: backward(s, k).wait_send())
            pl.when(a < outer - 1)(lambda s=s, k=k: chain(s, k).wait_send())
            result(s, k).wait_send()


def shards(n, states, slab_steps, offset, log_sigma, step_size, w_in, w_mid, w_out, embed):
    _, F, H, W = states.shape
    CH = w_in.shape[1]
    chips = n // 2
    inner = 1
    while 4 * inner * inner <= chips:
        inner *= 2
    FP = up(F, 16)
    K1 = up(3 * F, 128)
    K = H // 2
    x = jnp.transpose(states[0], (1, 0, 2))
    vmem = pl.BlockSpec(memory_space=pltpu.VMEM)
    smem = pl.BlockSpec(memory_space=pltpu.SMEM)
    hbm = pl.BlockSpec(memory_space=pl.ANY)
    bf16, f32 = jnp.bfloat16, jnp.float32
    slot = pltpu.VMEM((SWEEPS, K, F, W), f32)
    flops = SWEEPS * 2 * 9 * (2 * F * CH + CH * CH) * H * W
    out = pl.pallas_call(
        functools.partial(kernel, (n, inner, F, CH, H, W, FP)),
        out_shape=jax.ShapeDtypeStruct((H, F, W), f32),
        in_specs=[hbm, smem, smem, smem, smem, hbm, hbm, hbm, vmem],
        out_specs=vmem,
        scratch_shapes=[
            pltpu.VMEM(w_in.shape, bf16),
            pltpu.VMEM(w_out.shape, bf16),
            pltpu.VMEM((3 * CH, K1), bf16),
            pltpu.VMEM((3 * CH, 3 * CH), bf16),
            pltpu.VMEM((3 * FP, 3 * CH), bf16),
            pltpu.VMEM((CH, W), f32),
            pltpu.VMEM((H + 2, F, W), f32),
            pltpu.VMEM((H, K1, W), bf16),
            pltpu.VMEM((H + 2, CH, W), bf16),
            pltpu.VMEM((H + 2, CH, W), bf16),
            pltpu.VMEM((SWEEPS, H, F, W), f32),
            slot, slot, slot, slot, slot, slot, slot, slot, slot,
            pltpu.SemaphoreType.DMA((3,)),
            pltpu.SemaphoreType.DMA((9,)),
            pltpu.SemaphoreType.DMA((5, SWEEPS, K)),
            pltpu.SemaphoreType.DMA((5, SWEEPS, K)),
        ],
        compiler_params=pltpu.CompilerParams(
            collective_id=0, has_side_effects=True, vmem_limit_bytes=40 * 1024 * 1024
        ),
        cost_estimate=pl.CostEstimate(
            flops=flops, bytes_accessed=4 * 1024 * 1024, transcendentals=SWEEPS * 2 * CH * H * W
        ),
    )(x, slab_steps, offset, log_sigma, step_size, w_in, w_mid, w_out, embed.reshape(CH // 128, 128))
    return jnp.transpose(out, (1, 0, 2))[None]


def solution(mesh):
    in_specs = (
        P(("grp", "tm"), None, None, None),
        P(("grp", "tm")),
        P("grp"),
        P(),
        P(),
        P(),
        P(),
        P(),
        P(),
    )
    out_specs = P(("grp", "tm"), None, None, None)
    body = functools.partial(shards, mesh.shape["tm"])
    return jax.shard_map(body, mesh=mesh, in_specs=in_specs, out_specs=out_specs, check_vma=False)
```

```python
import functools

import jax
import jax.numpy as jnp
from jax import lax
from jax.experimental import pallas as pl
from jax.experimental.pallas import tpu as pltpu
from jax.sharding import PartitionSpec as P

SWEEPS = 2
CHIP_LAG = 2
CHAIN_LAG = 4
MESH = pl.DeviceIdType.MESH


def up(value, multiple):
    return (value + multiple - 1) // multiple * multiple


def kernel(dims, x_hbm, steps_ref, offset_ref, ls_hbm, ss_hbm, win_hbm, wmid_hbm, wout_hbm, emb_ref, out_ref,
           x_v, win_v, wout_v, w1, w2, w3, eb, xf, xc, u1, u2, inc,
           ra, rp, rs, re, rr, sf, sb, se, sr,
           ls_ref, ss_ref, load_sem, wmid_sem, small_sem, ssem, rsem):
    n, inner, F, CH, H, W, FP = dims
    outer = n // (2 * inner)
    K = H // 2
    me = lax.axis_index("tm")
    core = lax.rem(me, 2)
    chip = me // 2
    b = lax.rem(chip, inner)
    a = chip // inner
    partner = me + 1 - 2 * core
    b_next, b_prev = me + 2, me - 2
    a_next, a_prev = me + 2 * inner, me - 2 * inner

    loads = [
        pltpu.make_async_copy(x_hbm, x_v, load_sem.at[0]),
        pltpu.make_async_copy(win_hbm, win_v, load_sem.at[1]),
        pltpu.make_async_copy(wout_hbm, wout_v, load_sem.at[2]),
    ]
    for tap in range(9):
        ka, kb = tap // 3, tap % 3
        loads.append(
            pltpu.make_async_copy(
                wmid_hbm.at[tap], w2.at[pl.ds(kb * CH, CH), pl.ds(ka * CH, CH)], wmid_sem.at[tap]
            )
        )
    small = [
        pltpu.make_async_copy(src, dst, small_sem.at[i])
        for i, (src, dst) in enumerate(
            ((ls_hbm, ls_ref), (ss_hbm, ss_ref))
        )
    ]
    for copy in small:
        copy.start()
    loads[1].start()
    loads[0].start()
    for copy in loads[2:]:
        copy.start()

    @pl.when(b == 0)
    def _():
        rp[...] = jnp.zeros_like(rp)

    @pl.when(b == inner - 1)
    def _():
        rs[...] = jnp.zeros_like(rs)

    @pl.when(a == 0)
    def _():
        re[...] = jnp.zeros_like(re)

    barrier = pltpu.get_barrier_semaphore()

    def greet(device):
        pl.semaphore_signal(barrier, inc=1, device_id={"tm": device}, device_id_type=MESH)

    greet(partner)
    for there, device in ((b > 0, b_prev), (b < inner - 1, b_next), (a > 0, a_prev), (a < outer - 1, a_next)):
        pl.when(there)(functools.partial(greet, device))

    zero_row = jnp.zeros((CH, W), jnp.bfloat16)
    for edge in (0, H + 1):
        u1[edge] = zero_row
        u2[edge] = zero_row
        xf[edge] = jnp.zeros((F, W), jnp.float32)

    loads[1].wait()
    for kb in range(3):
        parts = [win_v[3 * ka + kb].astype(jnp.float32) for ka in range(3)]
        parts.append(jnp.zeros((w1.shape[1] - 3 * F, CH), jnp.float32))
        stacked = jnp.concatenate(parts, axis=0)
        w1[pl.ds(kb * CH, CH), :] = jnp.transpose(stacked).astype(jnp.bfloat16)
    for copy in small:
        copy.wait()
    table = ls_ref.shape[1]
    table_row = lax.rem(steps_ref[...] + offset_ref[...], jnp.full((1, 1), table, jnp.int32))
    chosen = lax.broadcasted_iota(jnp.int32, (1, table), 1) == table_row
    log_noise = jnp.sum(jnp.where(chosen, ls_ref[...], 0.0), axis=1, keepdims=True)
    step_len = jnp.sum(jnp.where(chosen, ss_ref[...], 0.0), axis=1, keepdims=True)
    first = jnp.where(me == 0, 1.0, 0.0).astype(jnp.float32)

    for block in range(CH // 128):
        row = emb_ref[pl.ds(block, 1), :] * log_noise
        eb[pl.ds(block * 128, 128), :] = jnp.transpose(jnp.broadcast_to(row, (128, 128)))
    loads[0].wait()
    for r in range(H):
        xf[r + 1] = x_v[pl.ds(r, F, stride=H), :]

    lane = lax.broadcasted_iota(jnp.int32, (1, W), 1)

    def combine(product, rows, base, j):
        cols = slice(j * W, (j + 1) * W)
        left = pltpu.roll(product[0:rows, cols], 1, axis=1)
        mid = product[base:base + rows, cols]
        right = pltpu.roll(product[2 * base:2 * base + rows, cols], W - 1, axis=1)
        return mid + jnp.where(lane == 0, 0.0, left) + jnp.where(lane == W - 1, 0.0, right)

    def silu(value):
        half = 0.5 * value
        return half * (1.0 + jnp.tanh(half))

    def stage(r):
        parts = [xf[r], xf[r + 1], xf[r + 2], jnp.zeros((w1.shape[1] - 3 * F, W), jnp.float32)]
        xc[r] = jnp.concatenate(parts, axis=0).astype(jnp.bfloat16)

    def conv1(k):
        r = 2 * k
        stage(r)
        stage(r + 1)
        z = jnp.concatenate([xc[r], xc[r + 1]], axis=1)
        product = jnp.dot(w1[...], z, preferred_element_type=jnp.float32)
        for j in range(2):
            u1[r + j + 1] = silu(combine(product, CH, CH, j) + eb[...]).astype(jnp.bfloat16)

    def taps(u, r):
        return jnp.concatenate(
            [jnp.concatenate([u[r + ka], u[r + ka + 1]], axis=1) for ka in range(3)], axis=0
        )

    def conv2(k):
        r = 2 * k
        product = jnp.dot(w2[...], taps(u1, r), preferred_element_type=jnp.float32)
        for j in range(2):
            u2[r + j + 1] = silu(combine(product, CH, CH, j)).astype(jnp.bfloat16)

    def conv3(s, k):
        r = 2 * k
        product = jnp.dot(w3[...], taps(u2, r), preferred_element_type=jnp.float32)
        for j in range(2):
            inc[s, r + j] = step_len * combine(product, F, FP, j) + first * xf[r + j + 1]

    def remote(kind, s, k, src, dst, device):
        return pltpu.make_async_remote_copy(
            src_ref=src,
            dst_ref=dst,
            send_sem=ssem.at[kind, s, k],
            recv_sem=rsem.at[kind, s, k],
            device_id={"tm": device},
            device_id_type=MESH,
        )

    def own(k):
        return 2 * k + core

    def other(k):
        return 2 * k + 1 - core

    def pair(s, k):
        return remote(0, s, k, inc.at[s, other(k)], ra.at[s, k], partner)

    def forward(s, k):
        return remote(1, s, k, sf.at[s, k], rp.at[s, k], b_next)

    def backward(s, k):
        return remote(2, s, k, sb.at[s, k], rs.at[s, k], b_prev)

    def chain(s, k):
        return remote(3, s, k, se.at[s, k], re.at[s, k], a_next)

    def result(s, k):
        return remote(4, s, k, sr.at[s, k], rr.at[s, k], partner)

    def send_pair(s, k):
        pair(s, k).start()

    def send_chip(s, k):
        pair(s, k).wait_recv()
        chip_sum = inc[s, own(k)] + ra[s, k]
        sf[s, k] = chip_sum
        sb[s, k] = chip_sum

        @pl.when(b == 0)
        def _():
            forward(s, k).start()

        @pl.when(b == inner - 1)
        def _():
            backward(s, k).start()

    def send_plane(s, k):
        middle = (b > 0) & (b < inner - 1)
        chip_sum = inc[s, own(k)] + ra[s, k]

        @pl.when(b > 0)
        def _():
            forward(s, k).wait_recv()

        if inner > 2:
            @pl.when(middle)
            def _():
                sf[s, k] = rp[s, k] + chip_sum
                forward(s, k).start()

        @pl.when(b < inner - 1)
        def _():
            backward(s, k).wait_recv()

        if inner > 2:
            @pl.when(middle)
            def _():
                sb[s, k] = rs[s, k] + chip_sum
                backward(s, k).start()

        @pl.when(a > 0)
        def _():
            chain(s, k).wait_recv()

        before = re[s, k] + rp[s, k]

        @pl.when(a < outer - 1)
        def _():
            se[s, k] = before + chip_sum + rs[s, k]
            chain(s, k).start()

        is_second = core.astype(jnp.float32)
        sr[s, k] = before + (1.0 - is_second) * inc[s, own(k)]
        result(s, k).start()
        finish(s, own(k), before + is_second * ra[s, k])

    def finish(s, r, before):
        if s + 1 < SWEEPS:
            xf[r + 1] = before + first * xf[r + 1]
        else:
            out_ref[r] = before + inc[s, r]

    def receive(s, k):
        result(s, k).wait_recv()
        finish(s, other(k), rr[s, k])

    early = K - CHAIN_LAG

    def compute(s, t):
        if t < K:
            conv1(t)
        if s == 0 and t == 0:
            for copy in loads[3:]:
                copy.wait()
        if 1 <= t <= K:
            conv2(t - 1)
        if s == 0 and t == 1:
            loads[2].wait()
            for tap in range(9):
                ka, kb = tap // 3, tap % 3
                padded = jnp.concatenate(
                    [wout_v[tap].astype(jnp.float32), jnp.zeros((FP - F, CH), jnp.float32)], axis=0
                )
                w3[pl.ds(kb * FP, FP), pl.ds(ka * CH, CH)] = padded.astype(jnp.bfloat16)
            count = 1 + (b > 0).astype(jnp.int32) + (b < inner - 1).astype(jnp.int32)
            count = count + (a > 0).astype(jnp.int32) + (a < outer - 1).astype(jnp.int32)
            pl.semaphore_wait(barrier, count)
        if t >= 2:
            conv3(s, t - 2)
            send_pair(s, t - 2)
            if t - 2 >= CHIP_LAG:
                send_chip(s, t - 2 - CHIP_LAG)
            if t - 2 >= CHAIN_LAG:
                k = t - 2 - CHAIN_LAG
                if s + 1 < SWEEPS:
                    pl.when(a == 0)(lambda: send_plane(s, k))
                else:
                    send_plane(s, k)

    for s in range(SWEEPS):
        for t in range(K + 2):
            if s > 0:
                if t == 0:
                    receive(s - 1, 0)
                    send_plane(s - 1, K - 3)
                    receive(s - 1, 1)
                else:
                    if K - 3 + t < K:
                        send_plane(s - 1, K - 3 + t)
                    if t + 1 < K:
                        receive(s - 1, t + 1)
            compute(s, t)
        for k in range(K - CHIP_LAG, K - 1):
            send_chip(s, k)
        last = s + 1 == SWEEPS
        if last:
            for k in range(early, K - 3):
                send_plane(s, k)
            send_chip(s, K - 1)
            for k in range(K - 3, K):
                send_plane(s, k)
                if k - 2 >= 0:
                    receive(s, k - 3)
            for k in range(K - 3, K):
                receive(s, k)
        else:
            for k in range(early, K - 3):
                pl.when(a == 0)(lambda k=k: send_plane(s, k))
            send_chip(s, K - 1)
            for k in range(K - 3):
                pl.when(a > 0)(lambda k=k: send_plane(s, k))

    for s in range(SWEEPS):
        for k in range(K):
            pair(s, k).wait_send()
            pl.when(b < inner - 1)(lambda s=s, k=k: forward(s, k).wait_send())
            pl.when(b > 0)(lambda s=s, k=k: backward(s, k).wait_send())
            pl.when(a < outer - 1)(lambda s=s, k=k: chain(s, k).wait_send())
            result(s, k).wait_send()


def shards(n, states, slab_steps, offset, log_sigma, step_size, w_in, w_mid, w_out, embed):
    _, F, H, W = states.shape
    CH = w_in.shape[1]
    chips = n // 2
    inner = 1
    while 4 * inner * inner <= chips:
        inner *= 2
    FP = up(F, 16)
    K1 = up(3 * F, 128)
    K = H // 2
    x = states.reshape(F * H, W)
    vmem = pl.BlockSpec(memory_space=pltpu.VMEM)
    hbm = pl.BlockSpec(memory_space=pl.ANY)
    bf16, f32 = jnp.bfloat16, jnp.float32
    slot = pltpu.VMEM((SWEEPS, K, F, W), f32)
    flops = SWEEPS * 2 * 9 * (2 * F * CH + CH * CH) * H * W
    out = pl.pallas_call(
        functools.partial(kernel, (n, inner, F, CH, H, W, FP)),
        out_shape=jax.ShapeDtypeStruct((H, F, W), f32),
        in_specs=[hbm, vmem, vmem, hbm, hbm, hbm, hbm, hbm, vmem],
        out_specs=vmem,
        scratch_shapes=[
            pltpu.VMEM((F * H, W), f32),
            pltpu.VMEM((9, F, CH), bf16),
            pltpu.VMEM(w_out.shape, bf16),
            pltpu.VMEM((3 * CH, K1), bf16),
            pltpu.VMEM((3 * CH, 3 * CH), bf16),
            pltpu.VMEM((3 * FP, 3 * CH), bf16),
            pltpu.VMEM((CH, W), f32),
            pltpu.VMEM((H + 2, F, W), f32),
            pltpu.VMEM((H, K1, W), bf16),
            pltpu.VMEM((H + 2, CH, W), bf16),
            pltpu.VMEM((H + 2, CH, W), bf16),
            pltpu.VMEM((SWEEPS, H, F, W), f32),
            slot, slot, slot, slot, slot, slot, slot, slot, slot,
            pltpu.VMEM((1, log_sigma.shape[0]), f32),
            pltpu.VMEM((1, step_size.shape[0]), f32),
            pltpu.SemaphoreType.DMA((3,)),
            pltpu.SemaphoreType.DMA((9,)),
            pltpu.SemaphoreType.DMA((2,)),
            pltpu.SemaphoreType.DMA((5, SWEEPS, K)),
            pltpu.SemaphoreType.DMA((5, SWEEPS, K)),
        ],
        compiler_params=pltpu.CompilerParams(
            collective_id=0, has_side_effects=True, vmem_limit_bytes=64 * 1024 * 1024
        ),
        cost_estimate=pl.CostEstimate(
            flops=flops, bytes_accessed=4 * 1024 * 1024, transcendentals=SWEEPS * 2 * CH * H * W
        ),
    )(x, slab_steps.reshape(1, 1), offset.reshape(1, 1), log_sigma.reshape(1, -1), step_size.reshape(1, -1), jnp.transpose(w_in, (0, 2, 1)), w_mid, w_out, embed.reshape(CH // 128, 128))
    return jnp.transpose(out, (1, 0, 2))[None]


def solution(mesh):
    in_specs = (
        P(("grp", "tm"), None, None, None),
        P(("grp", "tm")),
        P("grp"),
        P(),
        P(),
        P(),
        P(),
        P(),
        P(),
    )
    out_specs = P(("grp", "tm"), None, None, None)
    body = functools.partial(shards, mesh.shape["tm"])
    return jax.shard_map(body, mesh=mesh, in_specs=in_specs, out_specs=out_specs, check_vma=False)
```

```python
import functools

import jax
import jax.numpy as jnp
from jax import lax
from jax.experimental import pallas as pl
from jax.experimental.pallas import tpu as pltpu
from jax.sharding import PartitionSpec as P

SWEEPS = 2
CHIP_LAG = 1
CHAIN_LAG = 4
MESH = pl.DeviceIdType.MESH


def up(value, multiple):
    return (value + multiple - 1) // multiple * multiple


def kernel(dims, x_hbm, steps_ref, offset_ref, ls_hbm, ss_hbm, win_hbm, wmid_hbm, wout_hbm, emb_ref, out_ref,
           x_v, out_v, win_v, wout_v, w1, w2, w3, eb, xf, xc, u1, u2, inc,
           ra, rp, rs, re, rr, sf, sb, se, sr,
           ls_ref, ss_ref, load_sem, wmid_sem, small_sem, ssem, rsem):
    n, inner, F, CH, H, W, FP = dims
    outer = n // (2 * inner)
    K = H // 2
    me = lax.axis_index("tm")
    core = lax.rem(me, 2)
    chip = me // 2
    b = lax.rem(chip, inner)
    a = chip // inner
    partner = me + 1 - 2 * core
    b_next, b_prev = me + 2, me - 2
    a_next, a_prev = me + 2 * inner, me - 2 * inner

    loads = [
        pltpu.make_async_copy(x_hbm, x_v.at[pl.ds(0, F * H)], load_sem.at[0]),
        pltpu.make_async_copy(win_hbm, win_v, load_sem.at[1]),
        pltpu.make_async_copy(wout_hbm, wout_v, load_sem.at[2]),
    ]
    for tap in range(9):
        ka, kb = tap // 3, tap % 3
        loads.append(
            pltpu.make_async_copy(
                wmid_hbm.at[tap], w2.at[pl.ds(kb * CH, CH), pl.ds(ka * CH, CH)], wmid_sem.at[tap]
            )
        )
    small = [
        pltpu.make_async_copy(src, dst, small_sem.at[i])
        for i, (src, dst) in enumerate(
            ((ls_hbm, ls_ref), (ss_hbm, ss_ref))
        )
    ]
    for copy in small:
        copy.start()
    loads[1].start()
    loads[0].start()
    for copy in loads[2:]:
        copy.start()

    @pl.when(b == 0)
    def _():
        rp[...] = jnp.zeros_like(rp)

    @pl.when(b == inner - 1)
    def _():
        rs[...] = jnp.zeros_like(rs)

    @pl.when(a == 0)
    def _():
        re[...] = jnp.zeros_like(re)

    barrier = pltpu.get_barrier_semaphore()

    def greet(device):
        pl.semaphore_signal(barrier, inc=1, device_id={"tm": device}, device_id_type=MESH)

    greet(partner)
    for there, device in ((b > 0, b_prev), (b < inner - 1, b_next), (a > 0, a_prev), (a < outer - 1, a_next)):
        pl.when(there)(functools.partial(greet, device))

    zero_row = jnp.zeros((CH, W), jnp.bfloat16)
    for edge in (0, H + 1):
        u1[edge] = zero_row
        u2[edge] = zero_row
        xf[edge] = jnp.zeros((F, W), jnp.float32)

    loads[1].wait()
    for kb in range(3):
        parts = [win_v[3 * ka + kb].astype(jnp.float32) for ka in range(3)]
        parts.append(jnp.zeros((w1.shape[1] - 3 * F, CH), jnp.float32))
        stacked = jnp.concatenate(parts, axis=0)
        w1[pl.ds(kb * CH, CH), :] = jnp.transpose(stacked).astype(jnp.bfloat16)
    for copy in small:
        copy.wait()
    table = ls_ref.shape[1]
    table_row = lax.rem(steps_ref[...] + offset_ref[...], jnp.full((1, 1), table, jnp.int32))
    chosen = lax.broadcasted_iota(jnp.int32, (1, table), 1) == table_row
    log_noise = jnp.sum(jnp.where(chosen, ls_ref[...], 0.0), axis=1, keepdims=True)
    step_len = jnp.sum(jnp.where(chosen, ss_ref[...], 0.0), axis=1, keepdims=True)
    first = jnp.where(me == 0, 1.0, 0.0).astype(jnp.float32)

    for block in range(CH // 128):
        row = emb_ref[pl.ds(block, 1), :] * log_noise
        eb[pl.ds(block * 128, 128), :] = jnp.transpose(jnp.broadcast_to(row, (128, 128)))
    loads[0].wait()
    for r in range(H):
        xf[r + 1] = x_v[pl.ds(r, F, stride=H), :]

    lane = lax.broadcasted_iota(jnp.int32, (1, W), 1)

    def combine(product, rows, base, j):
        cols = slice(j * W, (j + 1) * W)
        left = pltpu.roll(product[0:rows, cols], 1, axis=1)
        mid = product[base:base + rows, cols]
        right = pltpu.roll(product[2 * base:2 * base + rows, cols], W - 1, axis=1)
        return mid + jnp.where(lane == 0, 0.0, left) + jnp.where(lane == W - 1, 0.0, right)

    def silu(value):
        half = 0.5 * value
        return half * (1.0 + jnp.tanh(half))

    def stage(r):
        parts = [xf[r], xf[r + 1], xf[r + 2], jnp.zeros((w1.shape[1] - 3 * F, W), jnp.float32)]
        xc[r] = jnp.concatenate(parts, axis=0).astype(jnp.bfloat16)

    def conv1(k):
        r = 2 * k
        stage(r)
        stage(r + 1)
        z = jnp.concatenate([xc[r], xc[r + 1]], axis=1)
        product = jnp.dot(w1[...], z, preferred_element_type=jnp.float32)
        for j in range(2):
            u1[r + j + 1] = silu(combine(product, CH, CH, j) + eb[...]).astype(jnp.bfloat16)

    def taps(u, r):
        return jnp.concatenate(
            [jnp.concatenate([u[r + ka], u[r + ka + 1]], axis=1) for ka in range(3)], axis=0
        )

    def conv2(k):
        r = 2 * k
        product = jnp.dot(w2[...], taps(u1, r), preferred_element_type=jnp.float32)
        for j in range(2):
            u2[r + j + 1] = silu(combine(product, CH, CH, j)).astype(jnp.bfloat16)

    def conv3(s, k):
        r = 2 * k
        product = jnp.dot(w3[...], taps(u2, r), preferred_element_type=jnp.float32)
        for j in range(2):
            inc[s, r + j] = step_len * combine(product, F, FP, j) + first * xf[r + j + 1]

    def remote(kind, s, k, src, dst, device):
        return pltpu.make_async_remote_copy(
            src_ref=src,
            dst_ref=dst,
            send_sem=ssem.at[kind, s, k],
            recv_sem=rsem.at[kind, s, k],
            device_id={"tm": device},
            device_id_type=MESH,
        )

    def own(k):
        return 2 * k + core

    def other(k):
        return 2 * k + 1 - core

    def pair(s, k):
        return remote(0, s, k, inc.at[s, other(k)], ra.at[s, k], partner)

    def forward(s, k):
        return remote(1, s, k, sf.at[s, k], rp.at[s, k], b_next)

    def backward(s, k):
        return remote(2, s, k, sb.at[s, k], rs.at[s, k], b_prev)

    def chain(s, k):
        return remote(3, s, k, se.at[s, k], re.at[s, k], a_next)

    def result(s, k):
        return remote(4, s, k, sr.at[s, k], rr.at[s, k], partner)

    def send_pair(s, k):
        pair(s, k).start()

    def send_chip(s, k):
        pair(s, k).wait_recv()
        chip_sum = inc[s, own(k)] + ra[s, k]
        sf[s, k] = chip_sum
        sb[s, k] = chip_sum

        @pl.when(b == 0)
        def _():
            forward(s, k).start()

        @pl.when(b == inner - 1)
        def _():
            backward(s, k).start()

    def send_plane(s, k):
        middle = (b > 0) & (b < inner - 1)
        chip_sum = inc[s, own(k)] + ra[s, k]

        @pl.when(b > 0)
        def _():
            forward(s, k).wait_recv()

        if inner > 2:
            @pl.when(middle)
            def _():
                sf[s, k] = rp[s, k] + chip_sum
                forward(s, k).start()

        @pl.when(b < inner - 1)
        def _():
            backward(s, k).wait_recv()

        if inner > 2:
            @pl.when(middle)
            def _():
                sb[s, k] = rs[s, k] + chip_sum
                backward(s, k).start()

        @pl.when(a > 0)
        def _():
            chain(s, k).wait_recv()

        before = re[s, k] + rp[s, k]

        @pl.when(a < outer - 1)
        def _():
            se[s, k] = before + chip_sum + rs[s, k]
            chain(s, k).start()

        is_second = core.astype(jnp.float32)
        sr[s, k] = before + (1.0 - is_second) * inc[s, own(k)]
        result(s, k).start()
        finish(s, own(k), before + is_second * ra[s, k])

    def finish(s, r, before):
        if s + 1 < SWEEPS:
            xf[r + 1] = before + first * xf[r + 1]
        else:
            out_v[pl.ds(r, F, stride=H), :] = before + inc[s, r]

    def receive(s, k):
        result(s, k).wait_recv()
        finish(s, other(k), rr[s, k])

    early = K - CHAIN_LAG

    def compute(s, t):
        if t < K:
            conv1(t)
        if s == 0 and t == 0:
            for copy in loads[3:]:
                copy.wait()
        if 1 <= t <= K:
            conv2(t - 1)
        if s == 0 and t == 1:
            loads[2].wait()
            for tap in range(9):
                ka, kb = tap // 3, tap % 3
                padded = jnp.concatenate(
                    [wout_v[tap].astype(jnp.float32), jnp.zeros((FP - F, CH), jnp.float32)], axis=0
                )
                w3[pl.ds(kb * FP, FP), pl.ds(ka * CH, CH)] = padded.astype(jnp.bfloat16)
            count = 1 + (b > 0).astype(jnp.int32) + (b < inner - 1).astype(jnp.int32)
            count = count + (a > 0).astype(jnp.int32) + (a < outer - 1).astype(jnp.int32)
            pl.semaphore_wait(barrier, count)
        if t >= 2:
            conv3(s, t - 2)
            send_pair(s, t - 2)
            if t - 2 >= CHIP_LAG:
                send_chip(s, t - 2 - CHIP_LAG)
            if t - 2 >= CHAIN_LAG:
                k = t - 2 - CHAIN_LAG
                if s + 1 < SWEEPS:
                    pl.when(a == 0)(lambda: send_plane(s, k))
                else:
                    send_plane(s, k)

    for s in range(SWEEPS):
        for t in range(K + 2):
            if s > 0:
                if t == 0:
                    receive(s - 1, 0)
                    send_plane(s - 1, K - 3)
                    receive(s - 1, 1)
                else:
                    if K - 3 + t < K:
                        send_plane(s - 1, K - 3 + t)
                    if t + 1 < K:
                        receive(s - 1, t + 1)
            compute(s, t)
        for k in range(K - CHIP_LAG, K - 1):
            send_chip(s, k)
        last = s + 1 == SWEEPS
        if last:
            for k in range(early, K - 3):
                send_plane(s, k)
            send_chip(s, K - 1)
            for k in range(K - 3, K):
                send_plane(s, k)
                if k - 2 >= 0:
                    receive(s, k - 3)
            for k in range(K - 3, K):
                receive(s, k)
        else:
            for k in range(early, K - 3):
                pl.when(a == 0)(lambda k=k: send_plane(s, k))
            send_chip(s, K - 1)
            for k in range(K - 3):
                pl.when(a > 0)(lambda k=k: send_plane(s, k))

    store = pltpu.make_async_copy(out_v.at[pl.ds(0, F * H)], out_ref, load_sem.at[3])
    store.start()
    for s in range(SWEEPS):
        for k in range(K):
            pair(s, k).wait_send()
            pl.when(b < inner - 1)(lambda s=s, k=k: forward(s, k).wait_send())
            pl.when(b > 0)(lambda s=s, k=k: backward(s, k).wait_send())
            pl.when(a < outer - 1)(lambda s=s, k=k: chain(s, k).wait_send())
            result(s, k).wait_send()
    store.wait()


def shards(n, states, slab_steps, offset, log_sigma, step_size, w_in, w_mid, w_out, embed):
    _, F, H, W = states.shape
    CH = w_in.shape[1]
    chips = n // 2
    inner = 1
    while 4 * inner * inner <= chips:
        inner *= 2
    FP = up(F, 16)
    K1 = up(3 * F, 128)
    K = H // 2
    x = states.reshape(F * H, W)
    vmem = pl.BlockSpec(memory_space=pltpu.VMEM)
    hbm = pl.BlockSpec(memory_space=pl.ANY)
    bf16, f32 = jnp.bfloat16, jnp.float32
    slot = pltpu.VMEM((SWEEPS, K, F, W), f32)
    flops = SWEEPS * 2 * 9 * (2 * F * CH + CH * CH) * H * W
    out = pl.pallas_call(
        functools.partial(kernel, (n, inner, F, CH, H, W, FP)),
        out_shape=jax.ShapeDtypeStruct((F * H, W), f32),
        in_specs=[hbm, vmem, vmem, hbm, hbm, hbm, hbm, hbm, vmem],
        out_specs=hbm,
        scratch_shapes=[
            pltpu.VMEM((up(F, 8) * H, W), f32),
            pltpu.VMEM((up(F, 8) * H, W), f32),
            pltpu.VMEM((9, F, CH), bf16),
            pltpu.VMEM(w_out.shape, bf16),
            pltpu.VMEM((3 * CH, K1), bf16),
            pltpu.VMEM((3 * CH, 3 * CH), bf16),
            pltpu.VMEM((3 * FP, 3 * CH), bf16),
            pltpu.VMEM((CH, W), f32),
            pltpu.VMEM((H + 2, F, W), f32),
            pltpu.VMEM((H, K1, W), bf16),
            pltpu.VMEM((H + 2, CH, W), bf16),
            pltpu.VMEM((H + 2, CH, W), bf16),
            pltpu.VMEM((SWEEPS, H, F, W), f32),
            slot, slot, slot, slot, slot, slot, slot, slot, slot,
            pltpu.VMEM((1, log_sigma.shape[0]), f32),
            pltpu.VMEM((1, step_size.shape[0]), f32),
            pltpu.SemaphoreType.DMA((4,)),
            pltpu.SemaphoreType.DMA((9,)),
            pltpu.SemaphoreType.DMA((2,)),
            pltpu.SemaphoreType.DMA((5, SWEEPS, K)),
            pltpu.SemaphoreType.DMA((5, SWEEPS, K)),
        ],
        compiler_params=pltpu.CompilerParams(
            collective_id=0, has_side_effects=True, vmem_limit_bytes=64 * 1024 * 1024
        ),
        cost_estimate=pl.CostEstimate(
            flops=flops, bytes_accessed=4 * 1024 * 1024, transcendentals=SWEEPS * 2 * CH * H * W
        ),
    )(x, slab_steps.reshape(1, 1), offset.reshape(1, 1), log_sigma.reshape(1, -1), step_size.reshape(1, -1), jnp.transpose(w_in, (0, 2, 1)), w_mid, w_out, embed.reshape(CH // 128, 128))
    return out.reshape(states.shape)


def solution(mesh):
    in_specs = (
        P(("grp", "tm"), None, None, None),
        P(("grp", "tm")),
        P("grp"),
        P(),
        P(),
        P(),
        P(),
        P(),
        P(),
    )
    out_specs = P(("grp", "tm"), None, None, None)
    body = functools.partial(shards, mesh.shape["tm"])
    return jax.shard_map(body, mesh=mesh, in_specs=in_specs, out_specs=out_specs, check_vma=False)
```
